512 devices in a mesh: corpus: 16 (over z), frow: 4 (over x), fcol: 8 (over y, core).
Axes of the slice: x: 4, y: 4, z: 16, core: 2. Of those that a mesh axis runs over, the one named last changes fastest.
Arguments:
- feature_slab: bfloat16 [32768, 4096], P('corpus', ('frow', 'fcol')), may hold values from -6 to 6
- test_preconditioned: bfloat16 [16384, 4096], P('corpus', ('frow', 'fcol')), may hold values from -0.09375 to 0.09375
- train_weight: float32 [32768], P('corpus'), may hold values from 0.1 to 1
- pair_tests: int32 [16, 16], P('corpus'), may hold values from 0 to 127, as said below
- pair_trains: int32 [16, 16], P('corpus'), may hold values from 0 to 15
- pair_counts: int32 [16], P('corpus'), may hold values from 4 to 16
Outputs:
- gram_upper: float32 [4096, 4, 1024], P(('frow', 'corpus'), None, 'fcol')
- pair_scores: float32 [16, 16, 128, 128], P('corpus', None, ('frow', 'fcol'))
The draws below stay inside these ranges and needn't reach their ends.
Inputs may be any that keep to these rules, and one draw needn't show every extreme that they name: `pair_tests`: test block g is rows g * 128 to g * 128 + 127 of test_preconditioned, held by corpus index g // 8. Among the first pair_counts[c] slots of row c, at most 2 name blocks held by one corpus index.
All inputs are finite; a program needn't handle non-finite values.
Results may differ from the reference program's by a relative error of at most 0.0003.
Values may be sent and summed in bfloat16 or wider, within the bound.
No kernel may reach another device: no remote copies, remote signals or barrier semaphores. Data moves between devices by JAX's collectives and lax.ppermute only.
A program may use at most 64 MiB of HBM per device.

```python
import math
import jax
import jax.numpy as jnp
from jax import lax

FEAT = 4096
TB = 128
TBLK_DEV = 8
PAIRS = 16
ROWS = 32768
TESTS = 16384
TRB = 16
CAP = 2
N_CORPUS = 16
N_FROW = 4


def owner_order(sub_key):
    return jax.random.permutation(sub_key, N_CORPUS)


def pair_table(base_key):
    count_key, order_key, owner_key, local_key, train_key, pick_key = jax.random.split(base_key, 6)
    fewest = max(1, PAIRS // 4)
    full_dev = jax.random.randint(pick_key, (), 0, N_CORPUS)
    low_dev = (full_dev + 1) % N_CORPUS
    dev_ids = jnp.arange(N_CORPUS)
    counts = jax.random.randint(count_key, (N_CORPUS,), fewest, PAIRS + 1)
    counts = jnp.where(dev_ids == full_dev, PAIRS, jnp.where(dev_ids == low_dev, fewest, counts)).astype(jnp.int32)
    slot_ids = jnp.arange(PAIRS)
    is_dead = slot_ids[None, :] >= counts[:, None]
    sort_keys = jax.random.randint(order_key, (N_CORPUS, PAIRS), 0, 1024) * PAIRS + slot_ids[None, :]
    sort_keys = sort_keys + is_dead.astype(jnp.int32) * (1024 * PAIRS)
    sort_order = jnp.argsort(sort_keys, axis=1, stable=True)
    live_rank = jnp.argsort(sort_order, axis=1, stable=True)
    owner_perms = jax.vmap(owner_order)(jax.random.split(owner_key, N_CORPUS))
    later_pos = 1 + (live_rank - CAP) % (N_CORPUS - 1)
    position = jnp.where(live_rank < CAP, 0, later_pos)
    owners = jnp.take_along_axis(owner_perms, position, axis=1)
    local_block = jax.random.randint(local_key, (N_CORPUS, PAIRS), 0, TBLK_DEV)
    test_ids = owners * TBLK_DEV + local_block
    train_ids = jax.random.randint(train_key, (N_CORPUS, PAIRS), 0, TRB)
    is_last = is_dead & (live_rank == PAIRS - 1)
    test_ids = jnp.where(is_last, N_CORPUS * TBLK_DEV - 1, test_ids).astype(jnp.int32)
    train_ids = jnp.where(is_last, TRB - 1, train_ids).astype(jnp.int32)
    return (test_ids, train_ids, counts)


def draw_pair_tests(key, part):
    return pair_table(key)[0]


def draw_pair_trains(key, part):
    return pair_table(key)[1]


def draw_pair_counts(key, part):
    return pair_table(key)[2]


def shard_levels(key, shape, shards, low, high):
    gain, own = 1.0, jax.random.fold_in(key, 6)
    for axis_at, parts in shards:
        draws = jnp.exp(jax.random.uniform(jax.random.fold_in(own, axis_at), (parts,), jnp.float32, low / len(shards), high / len(shards)))
        gain = gain * jnp.repeat(draws, shape[axis_at] // parts).reshape([-1 if axis == axis_at else 1 for axis in range(len(shape))])
    return gain


def normal_values(stream_key, shape, width, bound, cuts=(), held_as=jnp.bfloat16):
    drawn = width * jax.random.normal(stream_key, shape, jnp.float32)
    if cuts:
        drawn = drawn * shard_levels(stream_key, shape, cuts, -0.22, 0.18)
    return jnp.clip(drawn, -bound, bound).astype(held_as)


def setup_inputs(seed: int = 0) -> dict:
    key_of = jax.random.split(jax.random.key(seed), 7)
    feature_slab = normal_values(key_of[0], (ROWS, FEAT), 1.0, 6.0, ((0, 16), (1, 32)))
    test_preconditioned = normal_values(key_of[1], (TESTS, FEAT), FEAT ** -0.5, 0.09375, ((0, 16), (1, 32)))
    train_weight = jnp.clip(jnp.exp(math.log(1.0) - 2.3025851 * jax.random.uniform(key_of[2], (ROWS,), jnp.float32) ** shard_levels(key_of[2], (ROWS,), ((0, 16),), -0.2, 0.2)), 0.1, 1.0)
    pair_tests = draw_pair_tests(jax.random.fold_in(key_of[6], 71), 0)
    pair_trains = draw_pair_trains(jax.random.fold_in(key_of[6], 71), 0)
    pair_counts = draw_pair_counts(jax.random.fold_in(key_of[6], 71), 0)
    return {"feature_slab": feature_slab, "test_preconditioned": test_preconditioned, "train_weight": train_weight, "pair_tests": pair_tests, "pair_trains": pair_trains, "pair_counts": pair_counts}


def reference(feature_slab, test_preconditioned, train_weight, pair_tests, pair_trains, pair_counts):
    gram_full = jnp.dot(feature_slab.T, feature_slab, preferred_element_type=jnp.float32)
    gram_upper = (jnp.triu(gram_full) * (ROWS ** -0.5)).reshape(FEAT, N_FROW, FEAT // N_FROW)
    test_blocks = test_preconditioned.reshape(N_CORPUS * TBLK_DEV, TB, FEAT)
    train_blocks = feature_slab.reshape(N_CORPUS, TRB, TB, FEAT)
    block_weights = train_weight.reshape(N_CORPUS, TRB, TB)
    slot_ids = jnp.arange(PAIRS, dtype=jnp.int32)

    def score_index(inputs):
        test_ids, train_ids, pair_count, own_blocks, own_weights = inputs
        picked_tests = jnp.take(test_blocks, test_ids, axis=0).astype(jnp.float32)
        picked_train = jnp.take(own_blocks, train_ids, axis=0).astype(jnp.float32)
        raw_scores = jnp.einsum("pak,pbk->pab", picked_tests, picked_train)
        column_weights = jnp.take(own_weights, train_ids, axis=0)
        is_live = (slot_ids < pair_count).astype(jnp.float32)
        return raw_scores * column_weights[:, None, :] * is_live[:, None, None]

    pair_scores = lax.map(score_index, (pair_tests, pair_trains, pair_counts, train_blocks, block_weights))
    return gram_upper, pair_scores
```

```python
import functools

import jax
import jax.numpy as jnp
from jax import lax
from jax.experimental import pallas as pl
from jax.experimental.pallas import tpu as pltpu
from jax.sharding import PartitionSpec as P

TB = 128
PAIRS = 16
CAP = 2
CORES = 2


def gram_kernel(scale, steps, x_size, y_size, place, *refs):
    column_refs, row_refs = refs[:x_size], refs[x_size:x_size + CORES * y_size]
    out_ref, total = refs[-2:]
    step = pl.program_id(0)
    rows = jnp.concatenate([ref[...] for ref in row_refs], axis=1)
    columns = jnp.concatenate([ref[...] for ref in column_refs], axis=1)
    product = lax.dot_general(
        rows, columns, (((0,), (0,)), ((), ())), preferred_element_type=jnp.float32
    )

    @pl.when(step == 0)
    def _():
        total[...] = product

    @pl.when(step > 0)
    def _():
        total[...] += product

    @pl.when(step == steps - 1)
    def _():
        width = out_ref.shape[1] // x_size
        frow_at, y_at, core_at = place[0], place[1], place[2]
        row_iota = lax.broadcasted_iota(jnp.int32, (width, width), 0)
        column_iota = lax.broadcasted_iota(jnp.int32, (width, width), 1)
        for r in range(CORES * y_size):
            row_y = lax.rem(y_at + r // CORES, y_size)
            row_core = core_at if r % CORES == 0 else CORES - 1 - core_at
            row_at = (row_y * CORES + row_core) * width
            row_first = frow_at * (CORES * y_size * width) + row_at
            for c in range(x_size):
                column_at = lax.rem(frow_at + c, x_size)
                column_first = (
                    column_at * (CORES * y_size) + y_at * CORES + core_at
                ) * width
                keep = row_first + row_iota <= column_first + column_iota
                block = total[r * width:(r + 1) * width, c * width:(c + 1) * width]
                out_ref[
                    pl.ds(pl.multiple_of(row_at, width), width),
                    pl.ds(pl.multiple_of(column_at * width, width), width),
                ] = jnp.where(keep, block * scale, 0.0)


def gram_tile(columns, rows, place, scale):
    depth, width = columns[0].shape
    steps = 4
    x_size, y_size = len(columns), len(rows) // CORES
    shape = (len(rows) * width, x_size * width)
    block = pl.BlockSpec((depth // steps, width), lambda i, place: (i, 0))
    return pl.pallas_call(
        functools.partial(gram_kernel, scale, steps, x_size, y_size),
        out_shape=jax.ShapeDtypeStruct(shape, jnp.float32),
        grid_spec=pltpu.PrefetchScalarGridSpec(
            num_scalar_prefetch=1,
            grid=(steps,),
            in_specs=[block] * (len(columns) + len(rows)),
            out_specs=pl.BlockSpec(shape, lambda i, place: (0, 0)),
            scratch_shapes=[pltpu.VMEM(shape, jnp.float32)],
        ),
        compiler_params=pltpu.CompilerParams(vmem_limit_bytes=32 * 1024 * 1024),
        cost_estimate=pl.CostEstimate(
            flops=2 * depth * shape[0] * shape[1],
            bytes_accessed=2 * depth * (shape[0] + shape[1]) + 4 * shape[0] * shape[1],
            transcendentals=0,
        ),
    )(place, *columns, *rows)


def score_kernel(groups, table, tests_ref, trains_ref, out_ref):
    share = TB // groups
    per_step = 8 // share
    for first in range(0, PAIRS, per_step):
        parts = []
        for slot in range(first, first + per_step):
            scores = lax.dot_general(
                tests_ref[table[0, slot]],
                trains_ref[table[1, slot]],
                (((1,), (1,)), ((), ())),
                preferred_element_type=jnp.float32,
            )
            parts.append(scores.reshape(groups, share, TB))
        out_ref[:, share * first:share * (first + per_step), :] = jnp.concatenate(parts, axis=1)


def pair_partials(tests, trains, table, groups):
    shape = (groups, PAIRS * TB // groups, TB)
    return pl.pallas_call(
        functools.partial(score_kernel, groups),
        out_shape=jax.ShapeDtypeStruct(shape, jnp.float32),
        grid_spec=pltpu.PrefetchScalarGridSpec(
            num_scalar_prefetch=1,
            grid=(1,),
            in_specs=[
                pl.BlockSpec(tests.shape, lambda i, table: (0, 0, 0)),
                pl.BlockSpec(trains.shape, lambda i, table: (0, 0, 0)),
            ],
            out_specs=pl.BlockSpec(shape, lambda i, table: (0, 0, 0)),
        ),
        compiler_params=pltpu.CompilerParams(vmem_limit_bytes=32 * 1024 * 1024),
    )(table, tests, trains)


def shift(axis, by):
    size = lax.axis_size(axis)
    return [((at + by) % size, at) for at in range(size)]


def shards(feature_slab, test_preconditioned, train_weight, pair_tests, pair_trains, pair_counts):
    slab_rows, feat_width = feature_slab.shape
    row_groups = lax.axis_size("frow")
    col_groups = lax.axis_size("fcol")
    corpus_size = lax.axis_size("corpus")
    frow_at = lax.axis_index("frow")
    fcol_at = lax.axis_index("fcol")

    blocks_held = test_preconditioned.shape[0] // TB
    test_ids = pair_tests[0]
    train_ids = pair_trains[0]
    slot_ids = jnp.arange(PAIRS, dtype=jnp.int32)
    is_live = slot_ids < pair_counts[0]
    holder = test_ids // blocks_held
    same = (holder[:, None] == holder[None, :]) & is_live[None, :]
    rank = jnp.sum(same & (slot_ids[None, :] < slot_ids[:, None]), axis=1).astype(jnp.int32)
    place_at = holder * CAP + rank
    asked = is_live[:, None] & (place_at[:, None] == jnp.arange(corpus_size * CAP)[None, :])
    wants = jnp.sum(jnp.where(asked, (test_ids % blocks_held)[:, None], 0), axis=0)
    wanted = lax.all_to_all(
        wants.astype(jnp.int32).reshape(corpus_size, CAP), "corpus", 0, 0, tiled=True
    )

    columns = [feature_slab]
    for by in range(1, row_groups):
        columns.append(lax.ppermute(feature_slab, "frow", shift("frow", by)))
    rows = []
    swap = [(at, at ^ 1) for at in range(col_groups)]
    for by in range(col_groups // CORES):
        own = feature_slab
        if by:
            own = lax.ppermute(feature_slab, "fcol", shift("fcol", CORES * by))
        rows += [own, lax.ppermute(own, "fcol", swap)]
    place = jnp.stack([frow_at, fcol_at // CORES, fcol_at % CORES]).astype(jnp.int32)
    norm_scale = (slab_rows * corpus_size) ** (-0.5)
    tile = gram_tile(columns, rows, place, norm_scale)
    summed_tile = lax.psum_scatter(tile, "corpus", scatter_dimension=0, tiled=True)
    gram_upper = summed_tile.reshape(summed_tile.shape[0], row_groups, feat_width)

    test_blocks = test_preconditioned.reshape(blocks_held, TB, feat_width)
    picked = jnp.take(test_blocks, wanted.reshape(-1), axis=0, mode="clip")
    picked = picked.reshape(corpus_size, CAP * TB, feat_width)
    received = lax.all_to_all(picked, "corpus", 0, 0, tiled=True)
    received = received.reshape(corpus_size * CAP, TB, feat_width)
    table = jnp.stack([jnp.where(is_live, place_at, 0), train_ids]).astype(jnp.int32)
    groups = row_groups * col_groups
    partials = pair_partials(
        received, feature_slab.reshape(-1, TB, feat_width), table, groups
    )
    gathered = lax.all_to_all(partials, ("frow", "fcol"), 0, 0, tiled=True)
    summed = jnp.sum(gathered, axis=0).reshape(PAIRS, TB // groups, TB)
    column_weights = jnp.take(train_weight.reshape(-1, TB), train_ids, axis=0)
    pair_scores = (
        summed * column_weights[:, None, :] * is_live.astype(jnp.float32)[:, None, None]
    )
    return (gram_upper, pair_scores[None])


def solution(mesh):
    return jax.shard_map(
        shards,
        mesh=mesh,
        in_specs=(
            P("corpus", ("frow", "fcol")),
            P("corpus", ("frow", "fcol")),
            P("corpus"),
            P("corpus", None),
            P("corpus", None),
            P("corpus"),
        ),
        out_specs=(P(("frow", "corpus"), None, "fcol"), P("corpus", None, ("frow", "fcol"), None)),
        check_vma=False,
    )
```

```python
import functools

import jax
import jax.numpy as jnp
from jax import lax
from jax.experimental import pallas as pl
from jax.experimental.pallas import tpu as pltpu
from jax.sharding import PartitionSpec as P

TB = 128
PAIRS = 16
CAP = 2
CORES = 2
ID_ROWS = 16
VMEM_BYTES = 56 * 1024 * 1024


def gram_kernel(scale, x_size, place, rows_ref, *refs):
    out_ref = refs[-1]
    depth, width = rows_ref.shape[1], out_ref.shape[1]
    frow_at, fcol_at, col_groups = place[0], place[1], place[2]
    columns = jnp.concatenate([ref[...] for ref in refs[:-1]], axis=1)
    product = lax.dot_general(
        rows_ref[...], columns, (((0,), (0,)), ((), ())), preferred_element_type=jnp.float32
    )
    row_first = frow_at * col_groups * width + pl.program_id(0) * depth
    iota = [lax.broadcasted_iota(jnp.int32, (depth, width), axis) for axis in (0, 1)]
    for c in range(x_size):
        column_at = lax.rem(frow_at + c, x_size)
        column_first = (column_at * col_groups + fcol_at) * width
        keep = row_first + iota[0] <= column_first + iota[1]
        block = product[:, c * width:(c + 1) * width]
        out_ref[pl.ds(column_at, depth, stride=x_size), :] = jnp.where(keep, block * scale, 0.0)


def gram_tile(rows, columns, place, scale):
    depth, width = columns[0].shape
    x_size, panel = len(columns), rows.shape[1]
    step = 2 * width
    shape = (panel * x_size, width)
    return pl.pallas_call(
        functools.partial(gram_kernel, scale, x_size),
        out_shape=jax.ShapeDtypeStruct(shape, jnp.float32),
        grid_spec=pltpu.PrefetchScalarGridSpec(
            num_scalar_prefetch=1,
            grid=(panel // step,),
            in_specs=[pl.BlockSpec((depth, step), lambda i, place: (0, i))]
            + [pl.BlockSpec((depth, width), lambda i, place: (0, 0))] * x_size,
            out_specs=pl.BlockSpec((step * x_size, width), lambda i, place: (i, 0)),
        ),
        compiler_params=pltpu.CompilerParams(vmem_limit_bytes=VMEM_BYTES),
        cost_estimate=pl.CostEstimate(
            flops=32 * depth * shape[0] * width,
            bytes_accessed=2 * depth * (panel + x_size * width) + 4 * shape[0] * width,
            transcendentals=0,
        ),
    )(place, rows, *columns)


def offer_kernel(held, tests, trains, count, trains_ref, out_ref, places, seen, block_of, id_of):
    holders = out_ref.shape[0]
    lane = lax.broadcasted_iota(jnp.int32, (ID_ROWS, TB), 1)

    @pl.loop(0, holders)
    def _(h):
        seen[h] = 0
        for r in range(CAP):
            block_of[h, r] = 0
            id_of[h, r] = 0

    @pl.loop(0, PAIRS)
    def _(slot):
        places[0, slot] = 0

        @pl.when(slot < count[0])
        def _():
            holder = tests[0, slot] // held
            rank = seen[holder]
            block_of[holder, rank] = trains[0, slot]
            id_of[holder, rank] = tests[0, slot] - holder * held
            places[0, slot] = holder * CAP + rank
            seen[holder] = rank + 1

    for h in range(holders):
        ids = jnp.zeros((ID_ROWS, TB), jnp.int32)
        for r in range(CAP):
            out_ref[h, r * TB:(r + 1) * TB, :] = trains_ref[block_of[h, r]]
            ids = jnp.where(lane == r, id_of[h, r], ids)
        out_ref[h, CAP * TB:, :] = ids.astype(jnp.float32).astype(out_ref.dtype)


def offers(trains, pair_tests, pair_trains, pair_counts, holders, held):
    smem = pl.BlockSpec(memory_space=pltpu.SMEM)
    shape = (holders, CAP * TB + ID_ROWS, trains.shape[-1])
    return pl.pallas_call(
        functools.partial(offer_kernel, held),
        out_shape=(
            jax.ShapeDtypeStruct(shape, trains.dtype),
            jax.ShapeDtypeStruct((1, PAIRS), jnp.int32),
        ),
        in_specs=[smem] * 3 + [pl.BlockSpec(memory_space=pltpu.VMEM)],
        out_specs=(pl.BlockSpec(memory_space=pltpu.VMEM), smem),
        scratch_shapes=[pltpu.SMEM((holders,), jnp.int32)]
        + [pltpu.SMEM((holders, CAP), jnp.int32)] * 2,
    )(pair_tests, pair_trains, pair_counts, trains)


def score_kernel(groups, ids, core, offered_ref, tests_ref, send_ref, keep_ref):
    share = TB // groups
    for asker in range(offered_ref.shape[0]):
        sent, kept = [], []
        for r in range(CAP):
            scores = lax.dot_general(
                tests_ref[ids[asker, r]],
                offered_ref[asker, r * TB:(r + 1) * TB, :],
                (((1,), (1,)), ((), ())),
                preferred_element_type=jnp.float32,
            )
            scores = scores.reshape(groups // CORES, CORES, share, TB)
            first, second = scores[:, 0], scores[:, 1]
            kept.append(jnp.where(core[0] == 0, first, second))
            sent.append(jnp.where(core[0] == 0, second, first))
        rows = slice(asker * CAP * share, (asker + 1) * CAP * share)
        send_ref[:, rows, :] = jnp.concatenate(sent, axis=1)
        keep_ref[:, rows, :] = jnp.concatenate(kept, axis=1)


def pair_partials(offered, tests, ids, core, groups):
    askers = offered.shape[0]
    shape = (groups // CORES, askers * CAP * TB // groups, TB)
    out_block = pl.BlockSpec(shape, lambda i, ids, core: (0, 0, 0))
    return pl.pallas_call(
        functools.partial(score_kernel, groups),
        out_shape=[jax.ShapeDtypeStruct(shape, jnp.float32)] * 2,
        grid_spec=pltpu.PrefetchScalarGridSpec(
            num_scalar_prefetch=2,
            grid=(1,),
            in_specs=[
                pl.BlockSpec(offered.shape, lambda i, ids, core: (0, 0, 0)),
                pl.BlockSpec(tests.shape, lambda i, ids, core: (0, 0, 0)),
            ],
            out_specs=[out_block] * 2,
        ),
        compiler_params=pltpu.CompilerParams(vmem_limit_bytes=VMEM_BYTES),
    )(ids, core, offered, tests)


def weigh_kernel(places, trains, count, scores_ref, weights_ref, out_ref):
    for slot in range(PAIRS):
        scores = scores_ref[places[0, slot]]
        weights = weights_ref[pl.ds(trains[0, slot], 1), :]
        out_ref[slot] = jnp.where(slot < count[0], scores * weights, 0.0)


def weigh(scores, weights, places, pair_trains, pair_counts):
    smem = pl.BlockSpec(memory_space=pltpu.SMEM)
    vmem = pl.BlockSpec(memory_space=pltpu.VMEM)
    return pl.pallas_call(
        weigh_kernel,
        out_shape=jax.ShapeDtypeStruct((PAIRS,) + scores.shape[1:], jnp.float32),
        in_specs=[smem] * 3 + [vmem] * 2,
        out_specs=vmem,
    )(places, pair_trains, pair_counts, scores, weights)


def shift(axis, by):
    size = lax.axis_size(axis)
    return [((at + by) % size, at) for at in range(size)]


def shards(feature_slab, test_preconditioned, train_weight, pair_tests, pair_trains, pair_counts):
    slab_rows, feat_width = feature_slab.shape
    row_groups = lax.axis_size("frow")
    col_groups = lax.axis_size("fcol")
    corpus_size = lax.axis_size("corpus")
    frow_at = lax.axis_index("frow")
    fcol_at = lax.axis_index("fcol")

    held = test_preconditioned.shape[0] // TB
    offered, places = offers(
        feature_slab.reshape(-1, TB, feat_width), pair_tests, pair_trains, pair_counts, corpus_size, held
    )
    offered = lax.all_to_all(offered, "corpus", 0, 0, tiled=True)
    ids = offered[:, CAP * TB, :CAP].astype(jnp.int32)

    panel = lax.all_gather(feature_slab, "fcol", axis=1, tiled=True)
    columns = [feature_slab] + [
        lax.ppermute(feature_slab, "frow", shift("frow", by)) for by in range(1, row_groups)
    ]
    place = jnp.stack([frow_at, fcol_at, jnp.int32(col_groups)]).astype(jnp.int32)
    norm_scale = (slab_rows * corpus_size) ** (-0.5)
    tile = gram_tile(panel, columns, place, norm_scale)
    summed_tile = lax.psum_scatter(tile, "corpus", scatter_dimension=0, tiled=True)
    gram_upper = summed_tile.reshape(-1, row_groups, feat_width)

    groups = row_groups * col_groups
    core = (fcol_at % CORES).astype(jnp.int32).reshape(1)
    send, keep = pair_partials(
        offered, test_preconditioned.reshape(held, TB, feat_width), ids, core, groups
    )
    partials = keep + lax.ppermute(send, "fcol", [(at, at ^ 1) for at in range(col_groups)])
    same_core = [list(range(at, groups, CORES)) for at in range(CORES)]
    gathered = lax.all_to_all(
        partials, ("frow", "fcol"), 0, 0, axis_index_groups=same_core, tiled=True
    )
    summed = jnp.sum(gathered, axis=0)
    returned = lax.all_to_all(summed.reshape(corpus_size, -1, TB), "corpus", 0, 0, tiled=True)
    pair_scores = weigh(
        returned.reshape(corpus_size * CAP, TB // groups, TB),
        train_weight.reshape(-1, TB), places, pair_trains, pair_counts,
    )
    return (gram_upper, pair_scores[None])


def solution(mesh):
    return jax.shard_map(
        shards,
        mesh=mesh,
        in_specs=(
            P("corpus", ("frow", "fcol")),
            P("corpus", ("frow", "fcol")),
            P("corpus"),
            P("corpus", None),
            P("corpus", None),
            P("corpus"),
        ),
        out_specs=(P(("frow", "corpus"), None, "fcol"), P("corpus", None, ("frow", "fcol"), None)),
        check_vma=False,
    )
```

```python
import functools

import jax
import jax.numpy as jnp
from jax import lax
from jax.experimental import pallas as pl
from jax.experimental.pallas import tpu as pltpu
from jax.sharding import PartitionSpec as P

TB = 128
PAIRS = 16
CAP = 2
CORES = 2
ID_ROWS = 16
VMEM_BYTES = 56 * 1024 * 1024


def gram_kernel(scale, x_size, place, rows_ref, *refs):
    out_ref = refs[-1]
    depth, width = rows_ref.shape[1], out_ref.shape[1]
    frow_at, fcol_at, col_groups = place[0], place[1], place[2]
    columns = jnp.concatenate([ref[...] for ref in refs[:-1]], axis=1)
    product = lax.dot_general(
        rows_ref[...], columns, (((0,), (0,)), ((), ())), preferred_element_type=jnp.float32
    )
    row_first = frow_at * col_groups * width + pl.program_id(0) * depth
    iota = [lax.broadcasted_iota(jnp.int32, (depth, width), axis) for axis in (0, 1)]
    for c in range(x_size):
        column_at = lax.rem(frow_at + c, x_size)
        column_first = (column_at * col_groups + fcol_at) * width
        keep = row_first + iota[0] <= column_first + iota[1]
        block = product[:, c * width:(c + 1) * width]
        out_ref[pl.ds(column_at, depth, stride=x_size), :] = jnp.where(keep, block * scale, 0.0)


def gram_tile(rows, columns, place, scale):
    depth, width = columns[0].shape
    x_size, panel = len(columns), rows.shape[1]
    step = 4 * width
    shape = (panel * x_size, width)
    return pl.pallas_call(
        functools.partial(gram_kernel, scale, x_size),
        out_shape=jax.ShapeDtypeStruct(shape, jnp.float32),
        grid_spec=pltpu.PrefetchScalarGridSpec(
            num_scalar_prefetch=1,
            grid=(panel // step,),
            in_specs=[pl.BlockSpec((depth, step), lambda i, place: (0, i))]
            + [pl.BlockSpec((depth, width), lambda i, place: (0, 0))] * x_size,
            out_specs=pl.BlockSpec((step * x_size, width), lambda i, place: (i, 0)),
        ),
        compiler_params=pltpu.CompilerParams(vmem_limit_bytes=VMEM_BYTES),
        cost_estimate=pl.CostEstimate(
            flops=2 * depth * shape[0] * width,
            bytes_accessed=2 * depth * (panel + x_size * width) + 4 * shape[0] * width,
            transcendentals=0,
        ),
    )(place, rows, *columns)


def offer_kernel(held, tests, trains, count, trains_ref, out_ref, places, seen, block_of, id_of):
    holders = out_ref.shape[0]
    lane = lax.broadcasted_iota(jnp.int32, (ID_ROWS, TB), 1)

    @pl.loop(0, holders)
    def _(h):
        seen[h] = 0
        for r in range(CAP):
            block_of[h, r] = 0
            id_of[h, r] = 0

    @pl.loop(0, PAIRS)
    def _(slot):
        places[0, slot] = 0

        @pl.when(slot < count[0])
        def _():
            holder = tests[0, slot] // held
            rank = seen[holder]
            block_of[holder, rank] = trains[0, slot]
            id_of[holder, rank] = tests[0, slot] - holder * held
            places[0, slot] = holder * CAP + rank
            seen[holder] = rank + 1

    for h in range(holders):
        ids = jnp.zeros((ID_ROWS, TB), jnp.int32)
        for r in range(CAP):
            out_ref[h, r * TB:(r + 1) * TB, :] = trains_ref[block_of[h, r]]
            ids = jnp.where(lane == r, id_of[h, r], ids)
        out_ref[h, CAP * TB:, :] = ids.astype(jnp.float32).astype(out_ref.dtype)


def offers(trains, pair_tests, pair_trains, pair_counts, holders, held):
    smem = pl.BlockSpec(memory_space=pltpu.SMEM)
    shape = (holders, CAP * TB + ID_ROWS, trains.shape[-1])
    return pl.pallas_call(
        functools.partial(offer_kernel, held),
        out_shape=(
            jax.ShapeDtypeStruct(shape, trains.dtype),
            jax.ShapeDtypeStruct((1, PAIRS), jnp.int32),
        ),
        in_specs=[smem] * 3 + [pl.BlockSpec(memory_space=pltpu.VMEM)],
        out_specs=(pl.BlockSpec(memory_space=pltpu.VMEM), smem),
        scratch_shapes=[pltpu.SMEM((holders,), jnp.int32)]
        + [pltpu.SMEM((holders, CAP), jnp.int32)] * 2,
    )(pair_tests, pair_trains, pair_counts, trains)


def score_kernel(groups, ids, core, offered_ref, tests_ref, send_ref, keep_ref):
    share = TB // groups
    for asker in range(offered_ref.shape[0]):
        sent, kept = [], []
        for r in range(CAP):
            scores = lax.dot_general(
                tests_ref[ids[asker, r]],
                offered_ref[asker, r * TB:(r + 1) * TB, :],
                (((1,), (1,)), ((), ())),
                preferred_element_type=jnp.float32,
            )
            scores = scores.reshape(groups // CORES, CORES, share, TB)
            first, second = scores[:, 0], scores[:, 1]
            kept.append(jnp.where(core[0] == 0, first, second))
            sent.append(jnp.where(core[0] == 0, second, first))
        rows = slice(asker * CAP * share, (asker + 1) * CAP * share)
        send_ref[:, rows, :] = jnp.concatenate(sent, axis=1)
        keep_ref[:, rows, :] = jnp.concatenate(kept, axis=1)


def pair_partials(offered, tests, ids, core, groups):
    askers = offered.shape[0]
    shape = (groups // CORES, askers * CAP * TB // groups, TB)
    out_block = pl.BlockSpec(shape, lambda i, ids, core: (0, 0, 0))
    return pl.pallas_call(
        functools.partial(score_kernel, groups),
        out_shape=[jax.ShapeDtypeStruct(shape, jnp.float32)] * 2,
        grid_spec=pltpu.PrefetchScalarGridSpec(
            num_scalar_prefetch=2,
            grid=(1,),
            in_specs=[
                pl.BlockSpec(offered.shape, lambda i, ids, core: (0, 0, 0)),
                pl.BlockSpec(tests.shape, lambda i, ids, core: (0, 0, 0)),
            ],
            out_specs=[out_block] * 2,
        ),
        compiler_params=pltpu.CompilerParams(vmem_limit_bytes=VMEM_BYTES),
    )(ids, core, offered, tests)


def weigh_kernel(places, trains, count, scores_ref, weights_ref, out_ref):
    for slot in range(PAIRS):
        scores = scores_ref[places[0, slot]]
        weights = weights_ref[pl.ds(trains[0, slot], 1), :]
        out_ref[slot] = jnp.where(slot < count[0], scores * weights, 0.0)


def weigh(scores, weights, places, pair_trains, pair_counts):
    smem = pl.BlockSpec(memory_space=pltpu.SMEM)
    vmem = pl.BlockSpec(memory_space=pltpu.VMEM)
    return pl.pallas_call(
        weigh_kernel,
        out_shape=jax.ShapeDtypeStruct((PAIRS,) + scores.shape[1:], jnp.float32),
        in_specs=[smem] * 3 + [vmem] * 2,
        out_specs=vmem,
    )(places, pair_trains, pair_counts, scores, weights)


def shift(axis, by):
    size = lax.axis_size(axis)
    return [((at + by) % size, at) for at in range(size)]


def shards(feature_slab, test_preconditioned, train_weight, pair_tests, pair_trains, pair_counts):
    slab_rows, feat_width = feature_slab.shape
    row_groups = lax.axis_size("frow")
    col_groups = lax.axis_size("fcol")
    corpus_size = lax.axis_size("corpus")
    frow_at = lax.axis_index("frow")
    fcol_at = lax.axis_index("fcol")

    held = test_preconditioned.shape[0] // TB
    offered, places = offers(
        feature_slab.reshape(-1, TB, feat_width), pair_tests, pair_trains, pair_counts, corpus_size, held
    )
    offered = lax.all_to_all(offered, "corpus", 0, 0, tiled=True)
    ids = offered[:, CAP * TB, :CAP].astype(jnp.int32)

    panel = lax.all_gather(feature_slab, "fcol", axis=1, tiled=True)
    columns = [feature_slab] + [
        lax.ppermute(feature_slab, "frow", shift("frow", by)) for by in range(1, row_groups)
    ]
    place = jnp.stack([frow_at, fcol_at, jnp.int32(col_groups)]).astype(jnp.int32)
    norm_scale = (slab_rows * corpus_size) ** (-0.5)
    tile = gram_tile(panel, columns, place, norm_scale)
    summed_tile = lax.psum_scatter(tile, "corpus", scatter_dimension=0, tiled=True)
    gram_upper = summed_tile.reshape(-1, row_groups, feat_width)

    groups = row_groups * col_groups
    core = (fcol_at % CORES).astype(jnp.int32).reshape(1)
    send, keep = pair_partials(
        offered, test_preconditioned.reshape(held, TB, feat_width), ids, core, groups
    )
    partials = keep + lax.ppermute(send, "fcol", [(at, at ^ 1) for at in range(col_groups)])
    same_core = [list(range(at, groups, CORES)) for at in range(CORES)]
    gathered = lax.all_to_all(
        partials, ("frow", "fcol"), 0, 0, axis_index_groups=same_core, tiled=True
    )
    summed = jnp.sum(gathered, axis=0)
    returned = lax.all_to_all(summed.reshape(corpus_size, -1, TB), "corpus", 0, 0, tiled=True)
    pair_scores = weigh(
        returned.reshape(corpus_size * CAP, TB // groups, TB),
        train_weight.reshape(-1, TB), places, pair_trains, pair_counts,
    )
    return (gram_upper, pair_scores[None])


def solution(mesh):
    return jax.shard_map(
        shards,
        mesh=mesh,
        in_specs=(
            P("corpus", ("frow", "fcol")),
            P("corpus", ("frow", "fcol")),
            P("corpus"),
            P("corpus", None),
            P("corpus", None),
            P("corpus"),
        ),
        out_specs=(P(("frow", "corpus"), None, "fcol"), P("corpus", None, ("frow", "fcol"), None)),
        check_vma=False,
    )
```

```python
import functools

import jax
import jax.numpy as jnp
from jax import lax
from jax.experimental import pallas as pl
from jax.experimental.pallas import tpu as pltpu
from jax.sharding import PartitionSpec as P

TB = 128
PAIRS = 16
CAP = 2
CORES = 2
PAIR = 2
ID_ROWS = 16
VMEM_BYTES = 56 * 1024 * 1024


def gram_kernel(scale, x_size, place, rows_ref, *refs):
    out_ref = refs[-1]
    slices, _, width = rows_ref.shape
    frow_at, fcol_at, col_groups = place[0], place[1], place[2]
    columns = jnp.concatenate([ref[...] for ref in refs[:-1]], axis=1)
    depth = PAIR * width
    iota = [lax.broadcasted_iota(jnp.int32, (depth, width), axis) for axis in (0, 1)]
    for at in range(0, slices, PAIR):
        rows = jnp.concatenate([rows_ref[at + j] for j in range(PAIR)], axis=1)
        product = lax.dot_general(
            rows, columns, (((0,), (0,)), ((), ())), preferred_element_type=jnp.float32
        )
        row_first = (frow_at * col_groups + pl.program_id(0) * slices + at) * width
        for c in range(x_size):
            column_at = lax.rem(frow_at + c, x_size)
            column_first = (column_at * col_groups + fcol_at) * width
            keep = row_first + iota[0] <= column_first + iota[1]
            block = product[:, c * width:(c + 1) * width]
            out_ref[pl.ds(at * width * x_size + column_at, depth, stride=x_size), :] = jnp.where(
                keep, block * scale, 0.0
            )


def gram_tile(panel, columns, place, scale):
    depth, width = columns[0].shape
    x_size, slices = len(columns), panel.shape[0]
    step = slices // 2
    shape = (slices * width * x_size, width)
    return pl.pallas_call(
        functools.partial(gram_kernel, scale, x_size),
        out_shape=jax.ShapeDtypeStruct(shape, jnp.float32),
        grid_spec=pltpu.PrefetchScalarGridSpec(
            num_scalar_prefetch=1,
            grid=(slices // step,),
            in_specs=[pl.BlockSpec((step, depth, width), lambda i, place: (i, 0, 0))]
            + [pl.BlockSpec((depth, width), lambda i, place: (0, 0))] * x_size,
            out_specs=pl.BlockSpec((step * width * x_size, width), lambda i, place: (i, 0)),
        ),
        compiler_params=pltpu.CompilerParams(vmem_limit_bytes=VMEM_BYTES),
        cost_estimate=pl.CostEstimate(
            flops=2 * depth * shape[0] * width,
            bytes_accessed=2 * depth * (slices + x_size) * width + 4 * shape[0] * width,
            transcendentals=0,
        ),
    )(place, panel, *columns)


def offer_kernel(held, tests, trains, count, trains_ref, out_ref, places, seen, block_of, id_of):
    holders = out_ref.shape[0]
    lane = lax.broadcasted_iota(jnp.int32, (ID_ROWS, TB), 1)

    @pl.loop(0, holders)
    def _(h):
        seen[h] = 0
        for r in range(CAP):
            block_of[h, r] = 0
            id_of[h, r] = 0

    @pl.loop(0, PAIRS)
    def _(slot):
        places[0, slot] = 0

        @pl.when(slot < count[0])
        def _():
            holder = tests[0, slot] // held
            rank = seen[holder]
            block_of[holder, rank] = trains[0, slot]
            id_of[holder, rank] = tests[0, slot] - holder * held
            places[0, slot] = holder * CAP + rank
            seen[holder] = rank + 1

    for h in range(holders):
        ids = jnp.zeros((ID_ROWS, TB), jnp.int32)
        for r in range(CAP):
            out_ref[h, r * TB:(r + 1) * TB, :] = trains_ref[block_of[h, r]]
            ids = jnp.where(lane == r, id_of[h, r], ids)
        out_ref[h, CAP * TB:, :] = ids.astype(jnp.float32).astype(out_ref.dtype)


def offers(trains, pair_tests, pair_trains, pair_counts, holders, held):
    smem = pl.BlockSpec(memory_space=pltpu.SMEM)
    shape = (holders, CAP * TB + ID_ROWS, trains.shape[-1])
    return pl.pallas_call(
        functools.partial(offer_kernel, held),
        out_shape=(
            jax.ShapeDtypeStruct(shape, trains.dtype),
            jax.ShapeDtypeStruct((1, PAIRS), jnp.int32),
        ),
        in_specs=[smem] * 3 + [pl.BlockSpec(memory_space=pltpu.VMEM)],
        out_specs=(pl.BlockSpec(memory_space=pltpu.VMEM), smem),
        scratch_shapes=[pltpu.SMEM((holders,), jnp.int32)]
        + [pltpu.SMEM((holders, CAP), jnp.int32)] * 2,
    )(pair_tests, pair_trains, pair_counts, trains)


def score_kernel(groups, ids, core, offered_ref, tests_ref, send_ref, keep_ref):
    share = TB // groups
    for asker in range(offered_ref.shape[0]):
        sent, kept = [], []
        for r in range(CAP):
            scores = lax.dot_general(
                tests_ref[ids[asker, r]],
                offered_ref[asker, r * TB:(r + 1) * TB, :],
                (((1,), (1,)), ((), ())),
                preferred_element_type=jnp.float32,
            )
            scores = scores.reshape(groups // CORES, CORES, share, TB)
            first, second = scores[:, 0], scores[:, 1]
            kept.append(jnp.where(core[0] == 0, first, second))
            sent.append(jnp.where(core[0] == 0, second, first))
        rows = slice(asker * CAP * share, (asker + 1) * CAP * share)
        send_ref[:, rows, :] = jnp.concatenate(sent, axis=1)
        keep_ref[:, rows, :] = jnp.concatenate(kept, axis=1)


def pair_partials(offered, tests, ids, core, groups):
    askers = offered.shape[0]
    shape = (groups // CORES, askers * CAP * TB // groups, TB)
    out_block = pl.BlockSpec(shape, lambda i, ids, core: (0, 0, 0))
    return pl.pallas_call(
        functools.partial(score_kernel, groups),
        out_shape=[jax.ShapeDtypeStruct(shape, jnp.float32)] * 2,
        grid_spec=pltpu.PrefetchScalarGridSpec(
            num_scalar_prefetch=2,
            grid=(1,),
            in_specs=[
                pl.BlockSpec(offered.shape, lambda i, ids, core: (0, 0, 0)),
                pl.BlockSpec(tests.shape, lambda i, ids, core: (0, 0, 0)),
            ],
            out_specs=[out_block] * 2,
        ),
        compiler_params=pltpu.CompilerParams(vmem_limit_bytes=16 * 1024 * 1024),
    )(ids, core, offered, tests)


def weigh_kernel(places, trains, count, scores_ref, weights_ref, out_ref):
    for slot in range(PAIRS):
        scores = scores_ref[places[0, slot]]
        weights = weights_ref[pl.ds(trains[0, slot], 1), :]
        out_ref[slot] = jnp.where(slot < count[0], scores * weights, 0.0)


def weigh(scores, weights, places, pair_trains, pair_counts):
    smem = pl.BlockSpec(memory_space=pltpu.SMEM)
    vmem = pl.BlockSpec(memory_space=pltpu.VMEM)
    return pl.pallas_call(
        weigh_kernel,
        out_shape=jax.ShapeDtypeStruct((PAIRS,) + scores.shape[1:], jnp.float32),
        in_specs=[smem] * 3 + [vmem] * 2,
        out_specs=vmem,
    )(places, pair_trains, pair_counts, scores, weights)


def shift(axis, by):
    size = lax.axis_size(axis)
    return [((at + by) % size, at) for at in range(size)]


def shards(feature_slab, test_preconditioned, train_weight, pair_tests, pair_trains, pair_counts):
    slab_rows, feat_width = feature_slab.shape
    row_groups = lax.axis_size("frow")
    col_groups = lax.axis_size("fcol")
    corpus_size = lax.axis_size("corpus")
    frow_at = lax.axis_index("frow")
    fcol_at = lax.axis_index("fcol")

    held = test_preconditioned.shape[0] // TB
    offered, places = offers(
        feature_slab.reshape(-1, TB, feat_width), pair_tests, pair_trains, pair_counts, corpus_size, held
    )
    offered = lax.all_to_all(offered, "corpus", 0, 0, tiled=True)
    ids = offered[:, CAP * TB, :CAP].astype(jnp.int32)

    panel = lax.all_gather(feature_slab, "fcol")
    columns = [feature_slab]
    for by in reversed(range(1, row_groups)):
        pairs = [(source, to) for source, to in shift("frow", by) if source > to]
        columns.insert(1, lax.ppermute(feature_slab, "frow", pairs))
    place = jnp.stack([frow_at, fcol_at, jnp.int32(col_groups)]).astype(jnp.int32)
    norm_scale = (slab_rows * corpus_size) ** (-0.5)
    tile = gram_tile(panel, columns, place, norm_scale)
    summed_tile = lax.psum_scatter(tile, "corpus", scatter_dimension=0, tiled=True)
    gram_upper = summed_tile.reshape(-1, row_groups, feat_width)

    groups = row_groups * col_groups
    core = (fcol_at % CORES).astype(jnp.int32).reshape(1)
    send, keep = pair_partials(
        offered, test_preconditioned.reshape(held, TB, feat_width), ids, core, groups
    )
    partials = keep + lax.ppermute(send, "fcol", [(at, at ^ 1) for at in range(col_groups)])
    same_core = [list(range(at, groups, CORES)) for at in range(CORES)]
    gathered = lax.all_to_all(
        partials, ("frow", "fcol"), 0, 0, axis_index_groups=same_core, tiled=True
    )
    summed = jnp.sum(gathered, axis=0)
    returned = lax.all_to_all(summed.reshape(corpus_size, -1, TB), "corpus", 0, 0, tiled=True)
    pair_scores = weigh(
        returned.reshape(corpus_size * CAP, TB // groups, TB),
        train_weight.reshape(-1, TB), places, pair_trains, pair_counts,
    )
    return (gram_upper, pair_scores[None])


def solution(mesh):
    return jax.shard_map(
        shards,
        mesh=mesh,
        in_specs=(
            P("corpus", ("frow", "fcol")),
            P("corpus", ("frow", "fcol")),
            P("corpus"),
            P("corpus", None),
            P("corpus", None),
            P("corpus"),
        ),
        out_specs=(P(("frow", "corpus"), None, "fcol"), P("corpus", None, ("frow", "fcol"), None)),
        check_vma=False,
    )
```

```python
import functools

import jax
import jax.numpy as jnp
from jax import lax
from jax.experimental import pallas as pl
from jax.experimental.pallas import tpu as pltpu
from jax.sharding import PartitionSpec as P

TB = 128
PAIRS = 16
CAP = 2
CORES = 2
PAIR = 2
ID_ROWS = 16
VMEM_BYTES = 56 * 1024 * 1024


def gram_kernel(scale, x_size, place, panel_ref, *refs):
    out_ref, held, tile, arrived, left = refs[-5:]
    slices, _, width = held.shape
    frow_at, fcol_at, col_groups = place[0], place[1], place[2]
    arrivals = [
        pltpu.make_async_copy(panel_ref.at[at], held.at[at], arrived.at[at]) for at in range(slices)
    ]
    for copy in arrivals:
        copy.start()
    columns = jnp.concatenate([ref[...] for ref in refs[:-5]], axis=1)
    depth = PAIR * width
    iota = [lax.broadcasted_iota(jnp.int32, (depth, width), axis) for axis in (0, 1)]
    leaving = []
    for at in range(0, slices, PAIR):
        for copy in arrivals[at:at + PAIR]:
            copy.wait()
        rows = jnp.concatenate([held[at + j] for j in range(PAIR)], axis=1)
        product = lax.dot_general(
            rows, columns, (((0,), (0,)), ((), ())), preferred_element_type=jnp.float32
        )
        row_first = (frow_at * col_groups + at) * width
        for c in range(x_size):
            column_at = lax.rem(frow_at + c, x_size)
            column_first = (column_at * col_groups + fcol_at) * width
            keep = row_first + iota[0] <= column_first + iota[1]
            block = product[:, c * width:(c + 1) * width]
            tile[pl.ds(at * width * x_size + column_at, depth, stride=x_size), :] = jnp.where(
                keep, block * scale, 0.0
            )
        done = pl.ds(at * width * x_size, depth * x_size)
        leaving.append(pltpu.make_async_copy(tile.at[done], out_ref.at[done], left.at[at // PAIR]))
        leaving[-1].start()
    for copy in leaving:
        copy.wait()


def gram_tile(panel, columns, place, scale):
    depth, width = columns[0].shape
    x_size, slices = len(columns), panel.shape[0]
    shape = (slices * width * x_size, width)
    hbm = pl.BlockSpec(memory_space=pltpu.HBM)
    return pl.pallas_call(
        functools.partial(gram_kernel, scale, x_size),
        out_shape=jax.ShapeDtypeStruct(shape, jnp.float32),
        in_specs=[pl.BlockSpec(memory_space=pltpu.SMEM), hbm]
        + [pl.BlockSpec(memory_space=pltpu.VMEM)] * x_size,
        out_specs=hbm,
        scratch_shapes=[
            pltpu.VMEM(panel.shape, panel.dtype),
            pltpu.VMEM(shape, jnp.float32),
            pltpu.SemaphoreType.DMA((slices,)),
            pltpu.SemaphoreType.DMA((slices // PAIR,)),
        ],
        compiler_params=pltpu.CompilerParams(vmem_limit_bytes=48 * 1024 * 1024),
        cost_estimate=pl.CostEstimate(
            flops=2 * depth * shape[0] * width,
            bytes_accessed=2 * depth * (slices + x_size) * width + 4 * shape[0] * width,
            transcendentals=0,
        ),
    )(place, panel, *columns)


def offer_kernel(held, tests, trains, count, trains_ref, out_ref, places, seen, block_of, id_of):
    holders = out_ref.shape[0]
    lane = lax.broadcasted_iota(jnp.int32, (ID_ROWS, TB), 1)

    @pl.loop(0, holders)
    def _(h):
        seen[h] = 0
        for r in range(CAP):
            block_of[h, r] = 0
            id_of[h, r] = 0

    @pl.loop(0, PAIRS)
    def _(slot):
        places[0, slot] = 0

        @pl.when(slot < count[0])
        def _():
            holder = tests[0, slot] // held
            rank = seen[holder]
            block_of[holder, rank] = trains[0, slot]
            id_of[holder, rank] = tests[0, slot] - holder * held
            places[0, slot] = holder * CAP + rank
            seen[holder] = rank + 1

    for h in range(holders):
        ids = jnp.zeros((ID_ROWS, TB), jnp.int32)
        for r in range(CAP):
            out_ref[h, r * TB:(r + 1) * TB, :] = trains_ref[block_of[h, r]]
            ids = jnp.where(lane == r, id_of[h, r], ids)
        out_ref[h, CAP * TB:, :] = ids.astype(jnp.float32).astype(out_ref.dtype)


def offers(trains, pair_tests, pair_trains, pair_counts, holders, held):
    smem = pl.BlockSpec(memory_space=pltpu.SMEM)
    shape = (holders, CAP * TB + ID_ROWS, trains.shape[-1])
    return pl.pallas_call(
        functools.partial(offer_kernel, held),
        out_shape=(
            jax.ShapeDtypeStruct(shape, trains.dtype),
            jax.ShapeDtypeStruct((1, PAIRS), jnp.int32),
        ),
        in_specs=[smem] * 3 + [pl.BlockSpec(memory_space=pltpu.VMEM)],
        out_specs=(pl.BlockSpec(memory_space=pltpu.VMEM), smem),
        scratch_shapes=[pltpu.SMEM((holders,), jnp.int32)]
        + [pltpu.SMEM((holders, CAP), jnp.int32)] * 2,
    )(pair_tests, pair_trains, pair_counts, trains)


def score_kernel(groups, ids, core, offered_ref, tests_ref, send_ref, keep_ref):
    share = TB // groups
    for asker in range(offered_ref.shape[0]):
        sent, kept = [], []
        for r in range(CAP):
            scores = lax.dot_general(
                tests_ref[ids[asker, r]],
                offered_ref[asker, r * TB:(r + 1) * TB, :],
                (((1,), (1,)), ((), ())),
                preferred_element_type=jnp.float32,
            )
            scores = scores.reshape(groups // CORES, CORES, share, TB)
            first, second = scores[:, 0], scores[:, 1]
            kept.append(jnp.where(core[0] == 0, first, second))
            sent.append(jnp.where(core[0] == 0, second, first))
        rows = slice(asker * CAP * share, (asker + 1) * CAP * share)
        send_ref[:, rows, :] = jnp.concatenate(sent, axis=1)
        keep_ref[:, rows, :] = jnp.concatenate(kept, axis=1)


def pair_partials(offered, tests, ids, core, groups):
    askers = offered.shape[0]
    shape = (groups // CORES, askers * CAP * TB // groups, TB)
    out_block = pl.BlockSpec(shape, lambda i, ids, core: (0, 0, 0))
    return pl.pallas_call(
        functools.partial(score_kernel, groups),
        out_shape=[jax.ShapeDtypeStruct(shape, jnp.float32)] * 2,
        grid_spec=pltpu.PrefetchScalarGridSpec(
            num_scalar_prefetch=2,
            grid=(1,),
            in_specs=[
                pl.BlockSpec(offered.shape, lambda i, ids, core: (0, 0, 0)),
                pl.BlockSpec(tests.shape, lambda i, ids, core: (0, 0, 0)),
            ],
            out_specs=[out_block] * 2,
        ),
        compiler_params=pltpu.CompilerParams(vmem_limit_bytes=16 * 1024 * 1024),
    )(ids, core, offered, tests)


def weigh_kernel(places, trains, count, scores_ref, weights_ref, out_ref):
    for slot in range(PAIRS):
        scores = scores_ref[places[0, slot]]
        weights = weights_ref[pl.ds(trains[0, slot], 1), :]
        out_ref[slot] = jnp.where(slot < count[0], scores * weights, 0.0)


def weigh(scores, weights, places, pair_trains, pair_counts):
    smem = pl.BlockSpec(memory_space=pltpu.SMEM)
    vmem = pl.BlockSpec(memory_space=pltpu.VMEM)
    return pl.pallas_call(
        weigh_kernel,
        out_shape=jax.ShapeDtypeStruct((PAIRS,) + scores.shape[1:], jnp.float32),
        in_specs=[smem] * 3 + [vmem] * 2,
        out_specs=vmem,
    )(places, pair_trains, pair_counts, scores, weights)


def shift(axis, by):
    size = lax.axis_size(axis)
    return [((at + by) % size, at) for at in range(size)]


def shards(feature_slab, test_preconditioned, train_weight, pair_tests, pair_trains, pair_counts):
    slab_rows, feat_width = feature_slab.shape
    row_groups = lax.axis_size("frow")
    col_groups = lax.axis_size("fcol")
    corpus_size = lax.axis_size("corpus")
    frow_at = lax.axis_index("frow")
    fcol_at = lax.axis_index("fcol")

    held = test_preconditioned.shape[0] // TB
    offered, places = offers(
        feature_slab.reshape(-1, TB, feat_width), pair_tests, pair_trains, pair_counts, corpus_size, held
    )
    offered = lax.all_to_all(offered, "corpus", 0, 0, tiled=True)
    ids = offered[:, CAP * TB, :CAP].astype(jnp.int32)

    panel = lax.all_gather(feature_slab, "fcol")
    columns = [feature_slab]
    for by in reversed(range(1, row_groups)):
        pairs = [(source, to) for source, to in shift("frow", by) if source > to]
        columns.insert(1, lax.ppermute(feature_slab, "frow", pairs))
    place = jnp.stack([frow_at, fcol_at, jnp.int32(col_groups)]).astype(jnp.int32)
    norm_scale = (slab_rows * corpus_size) ** (-0.5)
    tile = gram_tile(panel, columns, place, norm_scale)
    summed_tile = lax.psum_scatter(tile, "corpus", scatter_dimension=0, tiled=True)
    gram_upper = summed_tile.reshape(-1, row_groups, feat_width)

    groups = row_groups * col_groups
    core = (fcol_at % CORES).astype(jnp.int32).reshape(1)
    send, keep = pair_partials(
        offered, test_preconditioned.reshape(held, TB, feat_width), ids, core, groups
    )
    partials = keep + lax.ppermute(send, "fcol", [(at, at ^ 1) for at in range(col_groups)])
    same_core = [list(range(at, groups, CORES)) for at in range(CORES)]
    gathered = lax.all_to_all(
        partials, ("frow", "fcol"), 0, 0, axis_index_groups=same_core, tiled=True
    )
    summed = jnp.sum(gathered, axis=0)
    returned = lax.all_to_all(summed.reshape(corpus_size, -1, TB), "corpus", 0, 0, tiled=True)
    pair_scores = weigh(
        returned.reshape(corpus_size * CAP, TB // groups, TB),
        train_weight.reshape(-1, TB), places, pair_trains, pair_counts,
    )
    return (gram_upper, pair_scores[None])


def solution(mesh):
    return jax.shard_map(
        shards,
        mesh=mesh,
        in_specs=(
            P("corpus", ("frow", "fcol")),
            P("corpus", ("frow", "fcol")),
            P("corpus"),
            P("corpus", None),
            P("corpus", None),
            P("corpus"),
        ),
        out_specs=(P(("frow", "corpus"), None, "fcol"), P("corpus", None, ("frow", "fcol"), None)),
        check_vma=False,
    )
```

```python
import functools

import jax
import jax.numpy as jnp
from jax import lax
from jax.experimental import pallas as pl
from jax.experimental.pallas import tpu as pltpu
from jax.sharding import PartitionSpec as P

TB = 128
PAIRS = 16
CAP = 2
CORES = 2
PAIR = 2
ID_ROWS = 16
VMEM_BYTES = 56 * 1024 * 1024


def gram_kernel(scale, x_size, cuts, place, panel_ref, *refs):
    out_ref, held, tile, arrived, left = refs[-5:]
    slices, _, width = held.shape
    frow_at, fcol_at, col_groups = place[0], place[1], place[2]
    arrivals = [
        pltpu.make_async_copy(panel_ref.at[at], held.at[at], arrived.at[at]) for at in range(slices)
    ]
    for copy in arrivals:
        copy.start()
    parts, strips = iter(refs[:-5]), []
    for count in cuts:
        strips.append(jnp.concatenate([next(parts)[...] for _ in range(count)], axis=0))
    columns = jnp.concatenate(strips, axis=1)
    depth = PAIR * width
    iota = [lax.broadcasted_iota(jnp.int32, (depth, width), axis) for axis in (0, 1)]
    leaving = []
    for at in range(0, slices, PAIR):
        for copy in arrivals[at:at + PAIR]:
            copy.wait()
        rows = jnp.concatenate([held[at + j] for j in range(PAIR)], axis=1)
        product = lax.dot_general(
            rows, columns, (((0,), (0,)), ((), ())), preferred_element_type=jnp.float32
        )
        row_first = (frow_at * col_groups + at) * width
        for c in range(x_size):
            column_at = lax.rem(frow_at + c, x_size)
            column_first = (column_at * col_groups + fcol_at) * width
            keep = row_first + iota[0] <= column_first + iota[1]
            block = product[:, c * width:(c + 1) * width]
            tile[pl.ds(at * width * x_size + column_at, depth, stride=x_size), :] = jnp.where(
                keep, block * scale, 0.0
            )
        done = pl.ds(at * width * x_size, depth * x_size)
        leaving.append(pltpu.make_async_copy(tile.at[done], out_ref.at[done], left.at[at // PAIR]))
        leaving[-1].start()
    for copy in leaving:
        copy.wait()


def gram_tile(panel, columns, place, scale):
    depth, width = columns[0][0].shape
    x_size, slices = len(columns), panel.shape[0]
    cuts = tuple(len(strip) for strip in columns)
    shape = (slices * width * x_size, width)
    hbm = pl.BlockSpec(memory_space=pltpu.HBM)
    return pl.pallas_call(
        functools.partial(gram_kernel, scale, x_size, cuts),
        out_shape=jax.ShapeDtypeStruct(shape, jnp.float32),
        in_specs=[pl.BlockSpec(memory_space=pltpu.SMEM), hbm]
        + [pl.BlockSpec(memory_space=pltpu.VMEM)] * sum(cuts),
        out_specs=hbm,
        scratch_shapes=[
            pltpu.VMEM(panel.shape, panel.dtype),
            pltpu.VMEM(shape, jnp.float32),
            pltpu.SemaphoreType.DMA((slices,)),
            pltpu.SemaphoreType.DMA((slices // PAIR,)),
        ],
        compiler_params=pltpu.CompilerParams(vmem_limit_bytes=48 * 1024 * 1024),
        cost_estimate=pl.CostEstimate(
            flops=2 * depth * shape[0] * width,
            bytes_accessed=2 * depth * (slices + x_size) * width + 4 * shape[0] * width,
            transcendentals=0,
        ),
    )(place, panel, *[part for strip in columns for part in strip])


def offer_kernel(held, tests, trains, count, trains_ref, out_ref, places, seen, block_of, id_of):
    holders = out_ref.shape[0]
    shift_by = held.bit_length() - 1
    live = count[0]
    for h in range(holders + 1):
        seen[h] = 0
    for at in range(holders * CAP):
        block_of[at] = 0
        id_of[at] = 0
    for slot in range(PAIRS):
        test = tests[0, slot]
        holder = jnp.where(slot < live, lax.shift_right_logical(test, shift_by), holders)
        rank = seen[holder]
        seen[holder] = rank + 1
        place = holder * CAP + rank
        block_of[place] = trains[0, slot]
        id_of[place] = lax.bitwise_and(test, held - 1)
        places[0, slot] = jnp.where(slot < live, place, 0)
    lane = lax.broadcasted_iota(jnp.int32, (ID_ROWS, TB), 1)
    for h in range(holders):
        ids = jnp.zeros((ID_ROWS, TB), jnp.int32)
        for r in range(CAP):
            out_ref[h, r * TB:(r + 1) * TB, :] = trains_ref[block_of[h * CAP + r]]
            ids = jnp.where(lane == r, id_of[h * CAP + r], ids)
        out_ref[h, CAP * TB:, :] = ids.astype(jnp.float32).astype(out_ref.dtype)


def offers(trains, pair_tests, pair_trains, pair_counts, holders, held):
    smem = pl.BlockSpec(memory_space=pltpu.SMEM)
    shape = (holders, CAP * TB + ID_ROWS, trains.shape[-1])
    return pl.pallas_call(
        functools.partial(offer_kernel, held),
        out_shape=(
            jax.ShapeDtypeStruct(shape, trains.dtype),
            jax.ShapeDtypeStruct((1, PAIRS), jnp.int32),
        ),
        in_specs=[smem] * 3 + [pl.BlockSpec(memory_space=pltpu.VMEM)],
        out_specs=(pl.BlockSpec(memory_space=pltpu.VMEM), smem),
        scratch_shapes=[pltpu.SMEM((holders + 1,), jnp.int32)]
        + [pltpu.SMEM((holders * CAP + PAIRS,), jnp.int32)] * 2,
    )(pair_tests, pair_trains, pair_counts, trains)


def score_kernel(groups, ids, core, offered_ref, tests_ref, send_ref, keep_ref):
    share = TB // groups
    for asker in range(offered_ref.shape[0]):
        sent, kept = [], []
        for r in range(CAP):
            scores = lax.dot_general(
                tests_ref[ids[asker, r]],
                offered_ref[asker, r * TB:(r + 1) * TB, :],
                (((1,), (1,)), ((), ())),
                preferred_element_type=jnp.float32,
            )
            scores = scores.reshape(groups // CORES, CORES, share, TB)
            first, second = scores[:, 0], scores[:, 1]
            kept.append(jnp.where(core[0] == 0, first, second))
            sent.append(jnp.where(core[0] == 0, second, first))
        rows = slice(asker * CAP * share, (asker + 1) * CAP * share)
        send_ref[:, rows, :] = jnp.concatenate(sent, axis=1)
        keep_ref[:, rows, :] = jnp.concatenate(kept, axis=1)


def pair_partials(offered, tests, ids, core, groups):
    askers = offered.shape[0]
    shape = (groups // CORES, askers * CAP * TB // groups, TB)
    out_block = pl.BlockSpec(shape, lambda i, ids, core: (0, 0, 0))
    return pl.pallas_call(
        functools.partial(score_kernel, groups),
        out_shape=[jax.ShapeDtypeStruct(shape, jnp.float32)] * 2,
        grid_spec=pltpu.PrefetchScalarGridSpec(
            num_scalar_prefetch=2,
            grid=(1,),
            in_specs=[
                pl.BlockSpec(offered.shape, lambda i, ids, core: (0, 0, 0)),
                pl.BlockSpec(tests.shape, lambda i, ids, core: (0, 0, 0)),
            ],
            out_specs=[out_block] * 2,
        ),
        compiler_params=pltpu.CompilerParams(vmem_limit_bytes=16 * 1024 * 1024),
    )(ids, core, offered, tests)


def weigh_kernel(places, trains, count, scores_ref, weights_ref, out_ref):
    for slot in range(PAIRS):
        scores = scores_ref[places[0, slot]]
        weights = weights_ref[pl.ds(trains[0, slot], 1), :]
        out_ref[slot] = jnp.where(slot < count[0], scores * weights, 0.0)


def weigh(scores, weights, places, pair_trains, pair_counts):
    smem = pl.BlockSpec(memory_space=pltpu.SMEM)
    vmem = pl.BlockSpec(memory_space=pltpu.VMEM)
    return pl.pallas_call(
        weigh_kernel,
        out_shape=jax.ShapeDtypeStruct((PAIRS,) + scores.shape[1:], jnp.float32),
        in_specs=[smem] * 3 + [vmem] * 2,
        out_specs=vmem,
    )(places, pair_trains, pair_counts, scores, weights)


def shift(axis, by):
    size = lax.axis_size(axis)
    return [((at + by) % size, at) for at in range(size)]


def shards(feature_slab, test_preconditioned, train_weight, pair_tests, pair_trains, pair_counts):
    slab_rows, feat_width = feature_slab.shape
    row_groups = lax.axis_size("frow")
    col_groups = lax.axis_size("fcol")
    corpus_size = lax.axis_size("corpus")
    frow_at = lax.axis_index("frow")
    fcol_at = lax.axis_index("fcol")

    held = test_preconditioned.shape[0] // TB
    assert held & (held - 1) == 0
    offered, places = offers(
        feature_slab.reshape(-1, TB, feat_width), pair_tests, pair_trains, pair_counts, corpus_size, held
    )
    offered = lax.all_to_all(offered, "corpus", 0, 0, tiled=True)
    ids = offered[:, CAP * TB, :CAP].astype(jnp.int32)

    panel = lax.all_gather(feature_slab, "fcol")
    half = slab_rows // 2

    def down(rows, by):
        pairs = [(source, to) for source, to in shift("frow", by) if source > to]
        return lax.ppermute(rows, "frow", pairs)

    columns = [[feature_slab], [down(feature_slab, 1)]]
    for by in range(2, row_groups):
        if by == 2 < row_groups - 1:
            columns.append([down(feature_slab[:half], by), down(columns[1][0][half:], 1)])
        else:
            columns.append([down(feature_slab, by)])
    place = jnp.stack([frow_at, fcol_at, jnp.int32(col_groups)]).astype(jnp.int32)
    norm_scale = (slab_rows * corpus_size) ** (-0.5)
    tile = gram_tile(panel, columns, place, norm_scale)
    summed_tile = lax.psum_scatter(tile, "corpus", scatter_dimension=0, tiled=True)
    gram_upper = summed_tile.reshape(-1, row_groups, feat_width)

    groups = row_groups * col_groups
    core = (fcol_at % CORES).astype(jnp.int32).reshape(1)
    send, keep = pair_partials(
        offered, test_preconditioned.reshape(held, TB, feat_width), ids, core, groups
    )
    partials = keep + lax.ppermute(send, "fcol", [(at, at ^ 1) for at in range(col_groups)])
    same_core = [list(range(at, groups, CORES)) for at in range(CORES)]
    gathered = lax.all_to_all(
        partials, ("frow", "fcol"), 0, 0, axis_index_groups=same_core, tiled=True
    )
    summed = jnp.sum(gathered, axis=0)
    returned = lax.all_to_all(summed.reshape(corpus_size, -1, TB), "corpus", 0, 0, tiled=True)
    pair_scores = weigh(
        returned.reshape(corpus_size * CAP, TB // groups, TB),
        train_weight.reshape(-1, TB), places, pair_trains, pair_counts,
    )
    return (gram_upper, pair_scores[None])


def solution(mesh):
    return jax.shard_map(
        shards,
        mesh=mesh,
        in_specs=(
            P("corpus", ("frow", "fcol")),
            P("corpus", ("frow", "fcol")),
            P("corpus"),
            P("corpus", None),
            P("corpus", None),
            P("corpus"),
        ),
        out_specs=(P(("frow", "corpus"), None, "fcol"), P("corpus", None, ("frow", "fcol"), None)),
        check_vma=False,
    )
```

```python
import functools

import jax
import jax.numpy as jnp
from jax import lax
from jax.experimental import pallas as pl
from jax.experimental.pallas import tpu as pltpu
from jax.sharding import PartitionSpec as P

TB = 128
PAIRS = 16
CAP = 2
CORES = 2
PAIR = 2
ID_ROWS = 16
VMEM_BYTES = 56 * 1024 * 1024


def gram_kernel(scale, x_size, cuts, place, panel_ref, *refs):
    out_ref, held, tile, arrived, left = refs[-5:]
    slices, _, width = held.shape
    frow_at, fcol_at, col_groups = place[0], place[1], place[2]
    arrivals = [
        pltpu.make_async_copy(panel_ref.at[at], held.at[at], arrived.at[at]) for at in range(slices)
    ]
    for copy in arrivals:
        copy.start()
    parts, strips = iter(refs[:-5]), []
    for count in cuts:
        strips.append(jnp.concatenate([next(parts)[...] for _ in range(count)], axis=0))
    columns = jnp.concatenate(strips, axis=1)
    depth = PAIR * width
    iota = [lax.broadcasted_iota(jnp.int32, (depth, width), axis) for axis in (0, 1)]
    leaving = []
    for at in range(0, slices, PAIR):
        for copy in arrivals[at:at + PAIR]:
            copy.wait()
        rows = jnp.concatenate([held[at + j] for j in range(PAIR)], axis=1)
        product = lax.dot_general(
            rows, columns, (((0,), (0,)), ((), ())), preferred_element_type=jnp.float32
        )
        row_first = (frow_at * col_groups + at) * width
        for c in range(x_size):
            column_at = lax.rem(frow_at + c, x_size)
            column_first = (column_at * col_groups + fcol_at) * width
            keep = row_first + iota[0] <= column_first + iota[1]
            block = product[:, c * width:(c + 1) * width]
            tile[pl.ds(at * width * x_size + column_at, depth, stride=x_size), :] = jnp.where(
                keep, block * scale, 0.0
            )
        done = pl.ds(at * width * x_size, depth * x_size)
        leaving.append(pltpu.make_async_copy(tile.at[done], out_ref.at[done], left.at[at // PAIR]))
        leaving[-1].start()
    for copy in leaving:
        copy.wait()


def gram_tile(panel, columns, place, scale):
    depth, width = columns[0][0].shape
    x_size, slices = len(columns), panel.shape[0]
    cuts = tuple(len(strip) for strip in columns)
    shape = (slices * width * x_size, width)
    hbm = pl.BlockSpec(memory_space=pltpu.HBM)
    return pl.pallas_call(
        functools.partial(gram_kernel, scale, x_size, cuts),
        out_shape=jax.ShapeDtypeStruct(shape, jnp.float32),
        in_specs=[pl.BlockSpec(memory_space=pltpu.SMEM), hbm]
        + [pl.BlockSpec(memory_space=pltpu.VMEM)] * sum(cuts),
        out_specs=hbm,
        scratch_shapes=[
            pltpu.VMEM(panel.shape, panel.dtype),
            pltpu.VMEM(shape, jnp.float32),
            pltpu.SemaphoreType.DMA((slices,)),
            pltpu.SemaphoreType.DMA((slices // PAIR,)),
        ],
        compiler_params=pltpu.CompilerParams(vmem_limit_bytes=48 * 1024 * 1024),
        cost_estimate=pl.CostEstimate(
            flops=2 * depth * shape[0] * width,
            bytes_accessed=2 * depth * (slices + x_size) * width + 4 * shape[0] * width,
            transcendentals=0,
        ),
    )(place, panel, *[part for strip in columns for part in strip])


def offer_kernel(held, tests, trains, count, trains_ref, out_ref, places, seen, block_of, id_of):
    holders = out_ref.shape[0]
    shift_by = held.bit_length() - 1
    live = count[0]
    for h in range(holders + 1):
        seen[h] = 0
    for at in range(holders * CAP):
        block_of[at] = 0
        id_of[at] = 0
    for slot in range(PAIRS):
        test = tests[0, slot]
        holder = jnp.where(slot < live, lax.shift_right_logical(test, shift_by), holders)
        rank = seen[holder]
        seen[holder] = rank + 1
        place = holder * CAP + rank
        block_of[place] = trains[0, slot]
        id_of[place] = lax.bitwise_and(test, held - 1)
        places[0, slot] = jnp.where(slot < live, place, 0)
    lane = lax.broadcasted_iota(jnp.int32, (ID_ROWS, TB), 1)
    blocks = [block_of[at] for at in range(holders * CAP)]
    asked = [id_of[at] for at in range(holders * CAP)]
    for h in range(holders):
        ids = jnp.zeros((ID_ROWS, TB), jnp.int32)
        for r in range(CAP):
            out_ref[h, r * TB:(r + 1) * TB, :] = trains_ref[blocks[h * CAP + r]]
            ids = jnp.where(lane == r, asked[h * CAP + r], ids)
        out_ref[h, CAP * TB:, :] = ids.astype(jnp.float32).astype(out_ref.dtype)


def offers(trains, pair_tests, pair_trains, pair_counts, holders, held):
    smem = pl.BlockSpec(memory_space=pltpu.SMEM)
    shape = (holders, CAP * TB + ID_ROWS, trains.shape[-1])
    return pl.pallas_call(
        functools.partial(offer_kernel, held),
        out_shape=(
            jax.ShapeDtypeStruct(shape, trains.dtype),
            jax.ShapeDtypeStruct((1, PAIRS), jnp.int32),
        ),
        in_specs=[smem] * 3 + [pl.BlockSpec(memory_space=pltpu.VMEM)],
        out_specs=(pl.BlockSpec(memory_space=pltpu.VMEM), smem),
        scratch_shapes=[pltpu.SMEM((holders + 1,), jnp.int32)]
        + [pltpu.SMEM((holders * CAP + PAIRS,), jnp.int32)] * 2,
    )(pair_tests, pair_trains, pair_counts, trains)


def score_kernel(groups, ids, core, offered_ref, tests_ref, send_ref, keep_ref):
    share = TB // groups
    for asker in range(offered_ref.shape[0]):
        sent, kept = [], []
        for r in range(CAP):
            scores = lax.dot_general(
                tests_ref[ids[asker, r]],
                offered_ref[asker, r * TB:(r + 1) * TB, :],
                (((1,), (1,)), ((), ())),
                preferred_element_type=jnp.float32,
            )
            scores = scores.reshape(groups // CORES, CORES, share, TB)
            first, second = scores[:, 0], scores[:, 1]
            kept.append(jnp.where(core[0] == 0, first, second))
            sent.append(jnp.where(core[0] == 0, second, first))
        rows = slice(asker * CAP * share, (asker + 1) * CAP * share)
        send_ref[:, rows, :] = jnp.concatenate(sent, axis=1)
        keep_ref[:, rows, :] = jnp.concatenate(kept, axis=1)


def pair_partials(offered, tests, ids, core, groups):
    askers = offered.shape[0]
    shape = (groups // CORES, askers * CAP * TB // groups, TB)
    out_block = pl.BlockSpec(shape, lambda i, ids, core: (0, 0, 0))
    return pl.pallas_call(
        functools.partial(score_kernel, groups),
        out_shape=[jax.ShapeDtypeStruct(shape, jnp.float32)] * 2,
        grid_spec=pltpu.PrefetchScalarGridSpec(
            num_scalar_prefetch=2,
            grid=(1,),
            in_specs=[
                pl.BlockSpec(offered.shape, lambda i, ids, core: (0, 0, 0)),
                pl.BlockSpec(tests.shape, lambda i, ids, core: (0, 0, 0)),
            ],
            out_specs=[out_block] * 2,
        ),
        compiler_params=pltpu.CompilerParams(vmem_limit_bytes=16 * 1024 * 1024),
    )(ids, core, offered, tests)


def weigh_kernel(places, trains, count, scores_ref, weights_ref, out_ref):
    for slot in range(PAIRS):
        scores = scores_ref[places[0, slot]]
        weights = weights_ref[pl.ds(trains[0, slot], 1), :]
        out_ref[slot] = jnp.where(slot < count[0], scores * weights, 0.0)


def weigh(scores, weights, places, pair_trains, pair_counts):
    smem = pl.BlockSpec(memory_space=pltpu.SMEM)
    vmem = pl.BlockSpec(memory_space=pltpu.VMEM)
    return pl.pallas_call(
        weigh_kernel,
        out_shape=jax.ShapeDtypeStruct((PAIRS,) + scores.shape[1:], jnp.float32),
        in_specs=[smem] * 3 + [vmem] * 2,
        out_specs=vmem,
        compiler_params=pltpu.CompilerParams(vmem_limit_bytes=8 * 1024 * 1024),
    )(places, pair_trains, pair_counts, scores, weights)


def shift(axis, by):
    size = lax.axis_size(axis)
    return [((at + by) % size, at) for at in range(size)]


def shards(feature_slab, test_preconditioned, train_weight, pair_tests, pair_trains, pair_counts):
    slab_rows, feat_width = feature_slab.shape
    row_groups = lax.axis_size("frow")
    col_groups = lax.axis_size("fcol")
    corpus_size = lax.axis_size("corpus")
    frow_at = lax.axis_index("frow")
    fcol_at = lax.axis_index("fcol")

    held = test_preconditioned.shape[0] // TB
    assert held & (held - 1) == 0
    offered, places = offers(
        feature_slab.reshape(-1, TB, feat_width), pair_tests, pair_trains, pair_counts, corpus_size, held
    )
    offered = lax.all_to_all(offered, "corpus", 0, 0, tiled=True)
    ids = offered[:, CAP * TB, :CAP].astype(jnp.int32)

    panel = lax.all_gather(feature_slab, "fcol")
    half = slab_rows // 2

    def down(rows, by):
        pairs = [(source, to) for source, to in shift("frow", by) if source > to]
        return lax.ppermute(rows, "frow", pairs)

    columns = [[feature_slab], [down(feature_slab, 1)]]
    for by in range(2, row_groups):
        if by == 2 < row_groups - 1:
            columns.append([down(feature_slab[:half], by), down(columns[1][0][half:], 1)])
        else:
            columns.append([down(feature_slab, by)])
    place = jnp.stack([frow_at, fcol_at, jnp.int32(col_groups)]).astype(jnp.int32)
    norm_scale = (slab_rows * corpus_size) ** (-0.5)
    tile = gram_tile(panel, columns, place, norm_scale)
    summed_tile = lax.psum_scatter(tile, "corpus", scatter_dimension=0, tiled=True)
    gram_upper = summed_tile.reshape(-1, row_groups, feat_width)

    groups = row_groups * col_groups
    core = (fcol_at % CORES).astype(jnp.int32).reshape(1)
    send, keep = pair_partials(
        offered, test_preconditioned.reshape(held, TB, feat_width), ids, core, groups
    )
    partials = keep + lax.ppermute(send, "fcol", [(at, at ^ 1) for at in range(col_groups)])
    same_core = [list(range(at, groups, CORES)) for at in range(CORES)]
    gathered = lax.all_to_all(
        partials, ("frow", "fcol"), 0, 0, axis_index_groups=same_core, tiled=True
    )
    summed = jnp.sum(gathered, axis=0)
    returned = lax.all_to_all(summed.reshape(corpus_size, -1, TB), "corpus", 0, 0, tiled=True)
    pair_scores = weigh(
        returned.reshape(corpus_size * CAP, TB // groups, TB),
        train_weight.reshape(-1, TB), places, pair_trains, pair_counts,
    )
    return (gram_upper, pair_scores[None])


def solution(mesh):
    return jax.shard_map(
        shards,
        mesh=mesh,
        in_specs=(
            P("corpus", ("frow", "fcol")),
            P("corpus", ("frow", "fcol")),
            P("corpus"),
            P("corpus", None),
            P("corpus", None),
            P("corpus"),
        ),
        out_specs=(P(("frow", "corpus"), None, "fcol"), P("corpus", None, ("frow", "fcol"), None)),
        check_vma=False,
    )
```
